32 devices in a mesh: groups: 2 (over x), row: 16 (over z, y, core).
Axes of the slice: x: 2, y: 2, z: 4, core: 2. Of those that a mesh axis runs over, the one named last changes fastest.
Arguments:
- features: float32 [8, 16384], P(None, ('groups', 'row')), parts along dimension 1, may hold values from 0 to 1
- inv_length: float32 [16], P('groups'), parts along dimension 0, may hold values from 3 to 6
- outscale: float32 [2], P('groups'), parts along dimension 0, may hold values from 0.5 to 2
- noise_var: float32 [2], P('groups'), parts along dimension 0, may hold values from 0.01 to 0.1
- solution: float32 [16, 16384], P(None, ('groups', 'row')), parts along dimension 1, may hold values from -6 to 6
- residual: float32 [16, 16384], P(None, ('groups', 'row')), parts along dimension 1, may hold values from -10 to 10
- direction: float32 [16, 16384], P(None, ('groups', 'row')), parts along dimension 1, may hold values from -10 to 10
Outputs:
- new_solution: float32 [16, 16384], P(None, ('groups', 'row')), parts along dimension 1
- new_residual: float32 [16, 16384], P(None, ('groups', 'row')), parts along dimension 1
- new_direction: float32 [16, 16384], P(None, ('groups', 'row')), parts along dimension 1
The draws below stay inside these ranges and needn't reach their ends.
There are 2 independent parts, one for each index of `groups`. The reference program is written for one: setup_inputs(seed, part) draws one part's arguments, and reference() takes and returns one part's arrays. A program takes and returns all parts, laid end to end along the dimension named above; each array names one. Nothing has to cross between parts.
All inputs are finite; a program needn't handle non-finite values.
Results may differ from the reference program's by a relative error of at most 0.00015.
Values sent between devices are 32-bit elements; how exact they have to be, the bound alone decides.
A program may use at most 64 MiB of HBM per device.

```python
import math
import jax
import jax.numpy as jnp
from jax import lax

FEATURES = 8
COLUMNS = 16
ROWS_DEV = 512
POINTS = 8192


def draw_residual(key, part):
    key = jax.random.fold_in(key, 11)
    position = jnp.arange(POINTS, dtype=jnp.float32) / POINTS
    ramp_scale = 0.6 * (1.0 + 2.0 * position)
    values = jax.random.truncated_normal(key, -5.0, 5.0, (COLUMNS, POINTS), jnp.float32)
    return values * ramp_scale[None, :]


def draw_direction(key, part):
    key = jax.random.fold_in(key, 12)
    position = jnp.arange(POINTS, dtype=jnp.float32) / POINTS
    ramp_scale = 0.6 * (1.0 + 2.0 * position)
    values = jax.random.truncated_normal(key, -5.0, 5.0, (COLUMNS, POINTS), jnp.float32)
    return values * ramp_scale[None, :]


def steps_of(rng, extent, split, least, top_value):
    factor_of, own = 1.0, jax.random.fold_in(rng, 6)
    for dim, parts in split:
        steps = jnp.exp(jax.random.uniform(jax.random.fold_in(own, dim), (parts,), jnp.float32, least / len(split), top_value / len(split)))
        factor_of = factor_of * jnp.repeat(steps, extent[dim] // parts).reshape([-1 if axis == dim else 1 for axis in range(len(extent))])
    return factor_of


def scatter_about(key, shape, deviation, most, pieces=(), kind=jnp.bfloat16):
    array = deviation * jax.random.normal(key, shape, jnp.float32)
    if pieces:
        array = array * steps_of(key, shape, pieces, -0.22, 0.18)
    return jnp.clip(array, -most, most).astype(kind)


def setup_inputs(seed: int = 0, part: int = 0) -> dict:
    streams_of = jax.random.split(jax.random.key(seed), 8)
    part_splits = jax.random.split(jax.random.fold_in(streams_of[7], part), 8)
    return {
        "features": jnp.clip(1.0 * jax.random.uniform(part_splits[0], (FEATURES, POINTS), jnp.float32) ** steps_of(part_splits[0], (FEATURES, POINTS), ((1, 16),), -0.2, 0.2), 0.0, 1.0),
        "inv_length": jnp.clip(jnp.exp(jax.random.uniform(part_splits[1], (FEATURES,), jnp.float32, math.log(3.0), math.log(6.0))), 3.0, 6.0),
        "outscale": jnp.clip(jnp.exp(jax.random.uniform(part_splits[2], (1,), jnp.float32, math.log(0.5), math.log(2.0))), 0.5, 2.0),
        "noise_var": jnp.clip(jnp.exp(jax.random.uniform(part_splits[3], (1,), jnp.float32, math.log(0.01), math.log(0.1))), 0.01, 0.1),
        "solution": scatter_about(part_splits[4], (COLUMNS, POINTS), 1.0, 6.0, ((1, 16),), jnp.float32),
        "residual": draw_residual(jax.random.fold_in(jax.random.fold_in(streams_of[7], part), 71), part),
        "direction": draw_direction(jax.random.fold_in(jax.random.fold_in(streams_of[7], part), 71), part),
    }


def kernel_block(zrow, zall, out_scale):
    cross_term = lax.dot_general(zrow, zall, (((0,), (0,)), ((), ())), precision=lax.Precision.HIGHEST, preferred_element_type=jnp.float32)
    dist_sq = lax.optimization_barrier(jnp.sum(zrow * zrow, 0))[:, None] + lax.optimization_barrier(jnp.sum(zall * zall, 0))[None, :] - 2.0 * cross_term
    scaled_dist = jnp.sqrt(5.0 * jnp.maximum(dist_sq, 0.0))
    return out_scale * (1.0 + scaled_dist + scaled_dist * scaled_dist / 3.0) * jnp.exp(-scaled_dist)

def reference(features, inv_length, outscale, noise_var, solution, residual, direction):
    scaled = features * inv_length[:, None]
    block_count = POINTS // ROWS_DEV
    stacked = scaled.reshape(FEATURES, block_count, ROWS_DEV).transpose(1, 0, 2)

    def one_block(zrow):
        kernel_tile = kernel_block(zrow, scaled, outscale[0])
        return lax.dot_general(direction, kernel_tile, (((1,), (1,)), ((), ())), precision=lax.Precision.HIGHEST, preferred_element_type=jnp.float32)
    block_terms = lax.map(one_block, stacked)
    image_sum = block_terms.transpose(1, 0, 2).reshape(COLUMNS, POINTS) + noise_var[0] * direction
    norm_old = lax.optimization_barrier(jnp.sum(residual * residual, 1))
    curvature = lax.optimization_barrier(jnp.sum(direction * image_sum, 1))
    step_size = norm_old / curvature
    new_solution = solution + step_size[:, None] * direction
    new_residual = residual - step_size[:, None] * image_sum
    norm_new = lax.optimization_barrier(jnp.sum(new_residual * new_residual, 1))
    new_direction = new_residual + (norm_new / norm_old)[:, None] * direction
    return (new_solution, new_residual, new_direction)
```

```python
import functools
import math

import jax
import jax.numpy as jnp
from jax import lax
from jax.experimental import pallas as pl
from jax.experimental.pallas import tpu as pltpu
from jax.sharding import PartitionSpec as P

LN2 = math.log(2.0)
FOLD = math.sqrt(5.0) / LN2
QUAD = LN2 * LN2 / 3.0
LIN = 3.0 / LN2
CONST = 3.0 / (LN2 * LN2)
TINY = 1e-30
CHUNK = 256


def rounded(x):
    return x.astype(jnp.bfloat16).astype(jnp.float32)


def pieces(x):
    first = rounded(x)
    rest = x - first
    second = rounded(rest)
    return first, second, rounded(rest - second)


def norm_rows(z, norm_first):
    n1, n2, n3 = pieces(jnp.sum(z * z, 0, keepdims=True))
    row = lax.broadcasted_iota(jnp.int32, z.shape, 0)
    at = 0 if norm_first else 3
    out = jnp.where((row < 3) if not norm_first else ((row >= 3) & (row < 6)), 1.0, 0.0)
    out = jnp.where(row == at, n1, out)
    out = jnp.where(row == at + 1, n2, out)
    return jnp.where(row == at + 2, n3, out)


def far_factor(z):
    z1, z2, z3 = pieces(z)
    return jnp.concatenate(
        [z1, z1, z2, z1, z3, z2, norm_rows(z, True), jnp.zeros_like(z)], 0
    ).astype(jnp.bfloat16)


def near_factor(z):
    z1, z2, z3 = (-2.0 * piece for piece in pieces(z))
    return jnp.concatenate(
        [z1, z2, z1, z3, z1, z2, norm_rows(z, False), jnp.zeros_like(z)], 0
    ).astype(jnp.bfloat16)


def step_kernel(
    n,
    depth,
    features,
    inv_length,
    outscale,
    noise_var,
    solution,
    residual,
    direction,
    new_solution,
    new_residual,
    new_direction,
    held,
    near,
    total,
    mine,
    sums,
    send_sem,
    recv_sem,
    sum_send,
    sum_recv,
):
    feats = features.shape[0]
    points = features.shape[1]
    columns = direction.shape[0]
    chips = n // 2
    half = chips // 2
    me = lax.axis_index("row")
    core = me % 2
    chip = me // 2
    y = chip % depth
    z = chip // depth
    span = chips // depth
    pos = y * span + z + (y % 2) * (span - 1 - 2 * z)

    def device_at(ring):
        ring = ring % chips
        yy = ring // span
        zz = ring % span
        zz = zz + (yy % 2) * (span - 1 - 2 * zz)
        return (zz * depth + yy) * 2 + core

    right = device_at(pos + 1)
    left = device_at(pos + chips - 1)
    sibling = me + 1 - 2 * core

    barrier = pltpu.get_barrier_semaphore()

    def greet(k, carry):
        pl.semaphore_signal(
            barrier, inc=1, device_id={"row": (me + k) % n}, device_id_type=pl.DeviceIdType.MESH
        )
        return carry

    lax.fori_loop(1, n, greet, 0)

    row = lax.broadcasted_iota(jnp.int32, (feats, points), 0)
    scale = jnp.zeros((feats, points), jnp.float32)
    for f in range(feats):
        scale = jnp.where(row == f, inv_length[f] * FOLD, scale)
    scaled = (features[...] - 0.5) * scale
    held[0, 0:feats, :] = scaled
    held[0, feats:, :] = direction[...]
    near[...] = near_factor(scaled)
    total[...] = jnp.zeros_like(total)

    pl.semaphore_wait(barrier, n - 1)

    def copy(source, slot, device):
        return pltpu.make_async_remote_copy(
            src_ref=held.at[source],
            dst_ref=held.at[slot],
            send_sem=send_sem.at[slot],
            recv_sem=recv_sem.at[slot],
            device_id={"row": device},
            device_id_type=pl.DeviceIdType.MESH,
        )

    def work(slot):
        block = held[slot]
        far = far_factor(block[0:feats])
        d = block[feats:]
        d_high = rounded(d)
        both = jnp.concatenate([d_high, d - d_high], 0).astype(jnp.bfloat16)
        out = None
        for at in range(0, points, CHUNK):
            dist = lax.dot_general(
                far[:, at : at + CHUNK],
                near[...],
                (((0,), (0,)), ((), ())),
                preferred_element_type=jnp.float32,
            )
            dist = jnp.maximum(dist, TINY)
            b = dist * lax.rsqrt(dist)
            tile = ((b + LIN) * b + CONST) * jnp.exp2(-b)
            high = tile.astype(jnp.bfloat16)
            low = (tile - high.astype(jnp.float32)).astype(jnp.bfloat16)
            lhs = both[:, at : at + CHUNK]
            part = jnp.dot(lhs, high, preferred_element_type=jnp.float32) + jnp.dot(
                lhs, low, preferred_element_type=jnp.float32
            )
            out = part if out is None else out + part
        total[...] += out

    copy(0, 2, right).start()
    copy(0, 4, left).start()
    copy(0, 1, sibling).start()

    def own_pair(k, carry):
        @pl.when(k == 1)
        def _():
            copy(0, 1, sibling).wait_recv()

        work(k)
        return carry

    lax.fori_loop(0, 2, own_pair, 0)

    def ring_step(s, carry):
        first = 2 + 4 * s
        second = first + 2
        copy(0, first, right).wait_recv()
        copy(0, second, left).wait_recv()

        @pl.when(s < half - 2)
        def _():
            copy(first, first + 4, right).start()
            copy(second, second + 4, left).start()

        @pl.when(s == half - 2)
        def _():
            copy(first + 2 * core, first + 4, right + core * (left - right)).start()

        copy(first, first + 1, sibling).start()
        copy(second, second + 1, sibling).start()

        def one(k, inner):
            slot = first + 2 * (k % 2) + k // 2

            @pl.when(k >= 2)
            def _():
                copy(0, slot, sibling).wait_recv()

            work(slot)
            return inner

        return lax.fori_loop(0, 4, one, carry)

    lax.fori_loop(0, half - 1, ring_step, 0)

    copy(0, n - 2, right).wait_recv()
    copy(n - 2, n - 1, sibling).start()

    def last_pair(k, carry):
        @pl.when(k == 1)
        def _():
            copy(0, n - 1, sibling).wait_recv()

        work(n - 2 + k)
        return carry

    lax.fori_loop(0, 2, last_pair, 0)

    d = direction[...]
    r = residual[...]
    image = (total[0:columns] + total[columns:]) * (outscale[0] * QUAD) + noise_var[0] * d
    lane = lax.broadcasted_iota(jnp.int32, (columns, 128), 1)
    sub = lax.broadcasted_iota(jnp.int32, (columns, 128), 0)
    spread = jnp.zeros((columns, 128), jnp.float32)
    for k, product in enumerate((r * r, d * image, r * image, image * image)):
        spread = jnp.where(lane == sub + k * columns, jnp.sum(product, 1, keepdims=True), spread)
    mine[...] = jnp.sum(spread, 0, keepdims=True)

    def sum_copy(k):
        return pltpu.make_async_remote_copy(
            src_ref=mine,
            dst_ref=sums.at[k],
            send_sem=sum_send.at[k],
            recv_sem=sum_recv.at[k],
            device_id={"row": (me + k) % n},
            device_id_type=pl.DeviceIdType.MESH,
        )

    def send_sum(k, carry):
        sum_copy(k).start()
        return carry

    lax.fori_loop(1, n, send_sum, 0)
    sums[0] = mine[...]

    def drain(k, carry):
        copy(0, k, sibling).wait_send()
        return carry

    lax.fori_loop(1, n, drain, 0)

    def take_sum(k, carry):
        sum_copy(k).wait()
        return carry

    lax.fori_loop(1, n, take_sum, 0)
    whole = jnp.broadcast_to(jnp.sum(sums[...], 0), (columns, 128))
    rr, curv, ri, ii = (
        jnp.sum(jnp.where(lane == sub + k * columns, whole, 0.0), 1, keepdims=True)
        for k in range(4)
    )
    alpha = rr / curv
    rr_new = jnp.maximum(rr - 2.0 * alpha * ri + alpha * alpha * ii, 0.0)
    fresh = r - alpha * image
    new_solution[...] = solution[...] + alpha * d
    new_residual[...] = fresh
    new_direction[...] = fresh + (rr_new / rr) * d


def shards(n, depth, features, inv_length, outscale, noise_var, solution, residual, direction):
    feats, points = features.shape
    columns = direction.shape[0]
    vmem = pl.BlockSpec(memory_space=pltpu.VMEM)
    smem = pl.BlockSpec(memory_space=pltpu.SMEM)
    out = jax.ShapeDtypeStruct(direction.shape, jnp.float32)
    return pl.pallas_call(
        functools.partial(step_kernel, n, depth),
        out_shape=(out, out, out),
        in_specs=[vmem, smem, smem, smem, vmem, vmem, vmem],
        out_specs=(vmem, vmem, vmem),
        scratch_shapes=[
            pltpu.VMEM((n, feats + columns, points), jnp.float32),
            pltpu.VMEM((8 * feats, points), jnp.bfloat16),
            pltpu.VMEM((2 * columns, points), jnp.float32),
            pltpu.VMEM((1, 128), jnp.float32),
            pltpu.VMEM((n, 1, 128), jnp.float32),
            pltpu.SemaphoreType.DMA((n,)),
            pltpu.SemaphoreType.DMA((n,)),
            pltpu.SemaphoreType.DMA((n,)),
            pltpu.SemaphoreType.DMA((n,)),
        ],
        compiler_params=pltpu.CompilerParams(
            collective_id=0, has_side_effects=True, vmem_limit_bytes=24 * 1024 * 1024
        ),
    )(features, inv_length, outscale, noise_var, solution, residual, direction)


def solution(mesh):
    n = mesh.shape["row"]
    depth = 1
    while 4 * depth * depth <= n // 2:
        depth *= 2
    whole = P(None, ("groups", "row"))
    part = P("groups")
    return jax.shard_map(
        functools.partial(shards, n, depth),
        mesh=mesh,
        in_specs=(whole, part, part, part, whole, whole, whole),
        out_specs=(whole, whole, whole),
        check_vma=False,
    )
```

```python
import functools
import math

import jax
import jax.numpy as jnp
from jax import lax
from jax.experimental import pallas as pl
from jax.experimental.pallas import tpu as pltpu
from jax.sharding import PartitionSpec as P

LN2 = math.log(2.0)
FOLD = math.sqrt(5.0) / LN2
QUAD = LN2 * LN2 / 3.0
LIN = 3.0 / LN2
CONST = 3.0 / (LN2 * LN2)
TINY = 1e-30


def rounded(x):
    return x.astype(jnp.bfloat16).astype(jnp.float32)


def pieces(x):
    first = rounded(x)
    rest = x - first
    second = rounded(rest)
    return first, second, rounded(rest - second)


def norm_rows(z, norm_first):
    n1, n2, n3 = pieces(jnp.sum(z * z, 0, keepdims=True))
    row = lax.broadcasted_iota(jnp.int32, z.shape, 0)
    at = 0 if norm_first else 3
    out = jnp.where((row < 3) if not norm_first else ((row >= 3) & (row < 6)), 1.0, 0.0)
    out = jnp.where(row == at, n1, out)
    out = jnp.where(row == at + 1, n2, out)
    return jnp.where(row == at + 2, n3, out)


def far_factor(z):
    z1, z2, z3 = pieces(z)
    return jnp.concatenate(
        [z1, z1, z2, z1, z3, z2, norm_rows(z, True), jnp.zeros_like(z)], 0
    ).astype(jnp.bfloat16)


def near_factor(z):
    z1, z2, z3 = (-2.0 * piece for piece in pieces(z))
    return jnp.concatenate(
        [z1, z2, z1, z3, z1, z2, norm_rows(z, False), jnp.zeros_like(z)], 0
    ).astype(jnp.bfloat16)


def step_kernel(
    n,
    depth,
    features_hbm,
    inv_length_hbm,
    outscale_hbm,
    noise_var_hbm,
    residual_hbm,
    direction_hbm,
    image_out,
    rates_out,
    features,
    inv_length,
    outscale,
    noise_var,
    residual,
    held,
    near,
    total,
    mine,
    sums,
    send_sem,
    recv_sem,
    sum_send,
    sum_recv,
    load_sem,
):
    feats, points = features.shape
    columns = residual.shape[0]
    direction = held.at[0, feats:]
    loads = [
        pltpu.make_async_copy(source, target, load_sem.at[k])
        for k, (source, target) in enumerate(
            (
                (features_hbm, features),
                (inv_length_hbm, inv_length),
                (direction_hbm, direction),
                (outscale_hbm, outscale),
                (noise_var_hbm, noise_var),
                (residual_hbm, residual),
            )
        )
    ]
    for load in loads:
        load.start()
    chips = n // 2
    half = chips // 2
    me = lax.axis_index("row")
    core = me % 2
    chip = me // 2
    y = chip % depth
    z = chip // depth
    span = chips // depth
    pos = y * span + z + (y % 2) * (span - 1 - 2 * z)

    def device_at(ring):
        ring = ring % chips
        yy = ring // span
        zz = ring % span
        zz = zz + (yy % 2) * (span - 1 - 2 * zz)
        return (zz * depth + yy) * 2 + core

    right = device_at(pos + 1)
    left = device_at(pos + chips - 1)
    sibling = me + 1 - 2 * core

    barrier = pltpu.get_barrier_semaphore()

    def greet(k, carry):
        pl.semaphore_signal(
            barrier, inc=1, device_id={"row": (me + k) % n}, device_id_type=pl.DeviceIdType.MESH
        )
        return carry

    lax.fori_loop(1, n, greet, 0)
    for load in loads[:3]:
        load.wait()

    row = lax.broadcasted_iota(jnp.int32, (feats, points), 0)
    scale = jnp.zeros((feats, points), jnp.float32)
    for f in range(feats):
        scale = jnp.where(row == f, inv_length[f] * FOLD, scale)
    scaled = (features[...] - 0.5) * scale
    held[0, 0:feats, :] = scaled
    near[...] = near_factor(scaled)
    total[...] = jnp.zeros_like(total)

    pl.semaphore_wait(barrier, n - 1)

    def copy(source, slot, device):
        return pltpu.make_async_remote_copy(
            src_ref=held.at[source],
            dst_ref=held.at[slot],
            send_sem=send_sem.at[slot],
            recv_sem=recv_sem.at[slot],
            device_id={"row": device},
            device_id_type=pl.DeviceIdType.MESH,
        )

    def work(slot, count):
        block = jnp.concatenate([held[slot + k] for k in range(count)], 1)
        far = far_factor(block[0:feats])
        d = block[feats:]
        d_high = rounded(d)
        both = jnp.concatenate([d_high, d - d_high], 0).astype(jnp.bfloat16)
        dist = lax.dot_general(
            far, near[...], (((0,), (0,)), ((), ())), preferred_element_type=jnp.float32
        )
        dist = jnp.maximum(dist, TINY)
        b = dist * lax.rsqrt(dist)
        tile = ((b + LIN) * b + CONST) * jnp.exp2(-b)
        high = tile.astype(jnp.bfloat16)
        low = (tile - high.astype(jnp.float32)).astype(jnp.bfloat16)
        total[...] += jnp.dot(both, high, preferred_element_type=jnp.float32) + jnp.dot(
            both, low, preferred_element_type=jnp.float32
        )

    copy(0, 2, right).start()
    copy(0, 3, left).start()
    copy(0, 1, sibling).start()

    def own_pair(k, carry):
        @pl.when(k == 1)
        def _():
            copy(0, 1, sibling).wait_recv()

        work(k, 1)
        return carry

    lax.fori_loop(0, 2, own_pair, 0)

    last = half * 2 - 2

    def pair(p, carry):
        first = 2 + 2 * p
        second = first + 1

        @pl.when((p % 2 == 0) & (p < last))
        def _():
            copy(0, first, right).wait_recv()
            copy(0, second, left).wait_recv()

            @pl.when(p < last - 2)
            def _():
                copy(first, first + 4, right).start()
                copy(second, second + 4, left).start()

            @pl.when(p == last - 2)
            def _():
                copy(first + core, first + 4, right + core * (left - right)).start()

            copy(first, first + 2, sibling).start()
            copy(second, second + 2, sibling).start()

        @pl.when(p % 2 == 1)
        def _():
            copy(0, first, sibling).wait_recv()
            copy(0, second, sibling).wait_recv()

        @pl.when(p == last)
        def _():
            copy(0, first, right).wait_recv()
            copy(first, second, sibling).start()
            copy(0, second, sibling).wait_recv()

        work(first, 2)
        return carry

    lax.fori_loop(0, last + 1, pair, 0)

    for load in loads[3:]:
        load.wait()
    d = direction[...]
    r = residual[...]
    image = (total[0:columns] + total[columns:]) * (outscale[0] * QUAD) + noise_var[0] * d
    lane = lax.broadcasted_iota(jnp.int32, (columns, 128), 1)
    sub = lax.broadcasted_iota(jnp.int32, (columns, 128), 0)
    spread = jnp.zeros((columns, 128), jnp.float32)
    for k, product in enumerate((r * r, d * image, r * image, image * image)):
        spread = jnp.where(lane == sub + k * columns, jnp.sum(product, 1, keepdims=True), spread)
    mine[...] = jnp.sum(spread, 0, keepdims=True)

    def sum_copy(k):
        return pltpu.make_async_remote_copy(
            src_ref=mine,
            dst_ref=sums.at[k],
            send_sem=sum_send.at[k],
            recv_sem=sum_recv.at[k],
            device_id={"row": (me + k) % n},
            device_id_type=pl.DeviceIdType.MESH,
        )

    def send_sum(k, carry):
        sum_copy(k).start()
        return carry

    lax.fori_loop(1, n, send_sum, 0)
    sums[0] = mine[...]

    def drain(k, carry):
        copy(0, k, sibling).wait_send()
        return carry

    lax.fori_loop(1, n, drain, 0)

    def take_sum(k, carry):
        sum_copy(k).wait()
        return carry

    lax.fori_loop(1, n, take_sum, 0)
    whole = jnp.broadcast_to(jnp.sum(sums[...], 0), (columns, 128))
    rr, curv, ri, ii = (
        jnp.sum(jnp.where(lane == sub + k * columns, whole, 0.0), 1, keepdims=True)
        for k in range(4)
    )
    alpha = rr / curv
    rr_new = jnp.maximum(rr - 2.0 * alpha * ri + alpha * alpha * ii, 0.0)
    image_out[...] = image
    rates_out[...] = jnp.where(lane == 0, alpha, rr_new / rr)


def shards(n, depth, features, inv_length, outscale, noise_var, solution, residual, direction):
    feats, points = features.shape
    columns = direction.shape[0]
    hbm = pl.BlockSpec(memory_space=pltpu.HBM)
    vmem = pl.BlockSpec(memory_space=pltpu.VMEM)
    image, rates = pl.pallas_call(
        functools.partial(step_kernel, n, depth),
        out_shape=(
            jax.ShapeDtypeStruct(direction.shape, jnp.float32),
            jax.ShapeDtypeStruct((columns, 128), jnp.float32),
        ),
        in_specs=[hbm] * 6,
        out_specs=(vmem, vmem),
        scratch_shapes=[
            pltpu.VMEM((feats, points), jnp.float32),
            pltpu.SMEM((feats,), jnp.float32),
            pltpu.SMEM((1,), jnp.float32),
            pltpu.SMEM((1,), jnp.float32),
            pltpu.VMEM((columns, points), jnp.float32),
            pltpu.VMEM((n, feats + columns, points), jnp.float32),
            pltpu.VMEM((8 * feats, points), jnp.bfloat16),
            pltpu.VMEM((2 * columns, points), jnp.float32),
            pltpu.VMEM((1, 128), jnp.float32),
            pltpu.VMEM((n, 1, 128), jnp.float32),
            pltpu.SemaphoreType.DMA((n,)),
            pltpu.SemaphoreType.DMA((n,)),
            pltpu.SemaphoreType.DMA((n,)),
            pltpu.SemaphoreType.DMA((n,)),
            pltpu.SemaphoreType.DMA((6,)),
        ],
        compiler_params=pltpu.CompilerParams(
            collective_id=0, has_side_effects=True, vmem_limit_bytes=32 * 1024 * 1024
        ),
    )(features, inv_length, outscale, noise_var, residual, direction)
    alpha, beta = rates[:, 0:1], rates[:, 1:2]
    new_residual = residual - alpha * image
    return solution + alpha * direction, new_residual, new_residual + beta * direction


def solution(mesh):
    n = mesh.shape["row"]
    depth = 1
    while 4 * depth * depth <= n // 2:
        depth *= 2
    whole = P(None, ("groups", "row"))
    part = P("groups")
    return jax.shard_map(
        functools.partial(shards, n, depth),
        mesh=mesh,
        in_specs=(whole, part, part, part, whole, whole, whole),
        out_specs=(whole, whole, whole),
        check_vma=False,
    )
```

```python
import functools
import math

import jax
import jax.numpy as jnp
from jax import lax
from jax.experimental import pallas as pl
from jax.experimental.pallas import tpu as pltpu
from jax.sharding import PartitionSpec as P

LN2 = math.log(2.0)
FOLD = math.sqrt(5.0) / LN2
QUAD = LN2 * LN2 / 3.0
LIN = 3.0 / LN2
CONST = 3.0 / (LN2 * LN2)
TINY = 1e-30


def rounded(x):
    return x.astype(jnp.bfloat16).astype(jnp.float32)


def pieces(x):
    first = rounded(x)
    rest = x - first
    second = rounded(rest)
    return first, second, rounded(rest - second)


def norm_rows(z, norm_first):
    n1, n2, n3 = pieces(jnp.sum(z * z, 0, keepdims=True))
    row = lax.broadcasted_iota(jnp.int32, z.shape, 0)
    at = 0 if norm_first else 3
    out = jnp.where((row < 3) if not norm_first else ((row >= 3) & (row < 6)), 1.0, 0.0)
    out = jnp.where(row == at, n1, out)
    out = jnp.where(row == at + 1, n2, out)
    return jnp.where(row == at + 2, n3, out)


def far_factor(z):
    z1, z2, z3 = pieces(z)
    return jnp.concatenate(
        [z1, z1, z2, z1, z3, z2, norm_rows(z, True), jnp.zeros_like(z)], 0
    ).astype(jnp.bfloat16)


def near_factor(z):
    z1, z2, z3 = (-2.0 * piece for piece in pieces(z))
    return jnp.concatenate(
        [z1, z2, z1, z3, z1, z2, norm_rows(z, False), jnp.zeros_like(z)], 0
    ).astype(jnp.bfloat16)


def step_kernel(
    n,
    depth,
    features_hbm,
    inv_length_hbm,
    outscale_hbm,
    noise_var_hbm,
    residual_hbm,
    direction_hbm,
    image_out,
    rates_out,
    features,
    inv_length,
    outscale,
    noise_var,
    residual,
    held,
    near,
    total,
    mine,
    sums,
    send_sem,
    recv_sem,
    sum_send,
    sum_recv,
    load_sem,
):
    feats, points = features.shape
    columns = residual.shape[0]
    direction = held.at[0, feats:]
    loads = [
        pltpu.make_async_copy(source, target, load_sem.at[k])
        for k, (source, target) in enumerate(
            (
                (features_hbm, features),
                (inv_length_hbm, inv_length),
                (direction_hbm, direction),
                (outscale_hbm, outscale),
                (noise_var_hbm, noise_var),
                (residual_hbm, residual),
            )
        )
    ]
    for load in loads:
        load.start()
    chips = n // 2
    half = chips // 2
    me = lax.axis_index("row")
    core = me % 2
    chip = me // 2
    y = chip % depth
    z = chip // depth
    span = chips // depth
    pos = y * span + z + (y % 2) * (span - 1 - 2 * z)

    def device_at(ring):
        ring = ring % chips
        yy = ring // span
        zz = ring % span
        zz = zz + (yy % 2) * (span - 1 - 2 * zz)
        return (zz * depth + yy) * 2 + core

    right = device_at(pos + 1)
    left = device_at(pos + chips - 1)
    sibling = me + 1 - 2 * core

    barrier = pltpu.get_barrier_semaphore()

    def greet(k, carry):
        pl.semaphore_signal(
            barrier, inc=1, device_id={"row": (me + k) % n}, device_id_type=pl.DeviceIdType.MESH
        )
        return carry

    lax.fori_loop(1, n, greet, 0)
    for load in loads[:3]:
        load.wait()

    row = lax.broadcasted_iota(jnp.int32, (feats, points), 0)
    scale = jnp.zeros((feats, points), jnp.float32)
    for f in range(feats):
        scale = jnp.where(row == f, inv_length[f] * FOLD, scale)
    scaled = (features[...] - 0.5) * scale
    held[0, 0:feats, :] = scaled
    near[...] = near_factor(scaled)
    total[...] = jnp.zeros_like(total)

    pl.semaphore_wait(barrier, n - 1)

    def copy(source, slot, device):
        return pltpu.make_async_remote_copy(
            src_ref=held.at[source],
            dst_ref=held.at[slot],
            send_sem=send_sem.at[slot],
            recv_sem=recv_sem.at[slot],
            device_id={"row": device},
            device_id_type=pl.DeviceIdType.MESH,
        )

    def work(slot, count):
        block = jnp.concatenate([held[slot + k] for k in range(count)], 1)
        far = far_factor(block[0:feats])
        d = block[feats:]
        d_high = rounded(d)
        both = jnp.concatenate([d_high, d - d_high], 0).astype(jnp.bfloat16)
        dist = lax.dot_general(
            far, near[...], (((0,), (0,)), ((), ())), preferred_element_type=jnp.float32
        )
        dist = jnp.maximum(dist, TINY)
        b = dist * lax.rsqrt(dist)
        tile = ((b + LIN) * b + CONST) * jnp.exp2(-b)
        high = tile.astype(jnp.bfloat16)
        low = (tile - high.astype(jnp.float32)).astype(jnp.bfloat16)
        total[...] += jnp.dot(both, high, preferred_element_type=jnp.float32)
        total[0:columns] += jnp.dot(both[0:columns], low, preferred_element_type=jnp.float32)

    copy(0, 2, right).start()
    copy(0, 3, left).start()
    copy(0, 1, sibling).start()

    def own_pair(k, carry):
        @pl.when(k == 1)
        def _():
            copy(0, 1, sibling).wait_recv()

        work(k, 1)
        return carry

    lax.fori_loop(0, 2, own_pair, 0)

    last = half * 2 - 2

    def pair(p, carry):
        first = 2 + 2 * p
        second = first + 1

        @pl.when((p % 2 == 0) & (p < last))
        def _():
            copy(0, first, right).wait_recv()
            copy(0, second, left).wait_recv()

            @pl.when(p < last - 2)
            def _():
                copy(first, first + 4, right).start()
                copy(second, second + 4, left).start()

            @pl.when(p == last - 2)
            def _():
                copy(first + core, first + 4, right + core * (left - right)).start()

            copy(first, first + 2, sibling).start()
            copy(second, second + 2, sibling).start()

        @pl.when(p % 2 == 1)
        def _():
            copy(0, first, sibling).wait_recv()
            copy(0, second, sibling).wait_recv()

        @pl.when(p == last)
        def _():
            copy(0, first, right).wait_recv()
            copy(first, second, sibling).start()
            copy(0, second, sibling).wait_recv()

        work(first, 2)
        return carry

    lax.fori_loop(0, last + 1, pair, 0)

    for load in loads[3:]:
        load.wait()
    d = direction[...]
    r = residual[...]
    image = (total[0:columns] + total[columns:]) * (outscale[0] * QUAD) + noise_var[0] * d
    lane = lax.broadcasted_iota(jnp.int32, (columns, 128), 1)
    sub = lax.broadcasted_iota(jnp.int32, (columns, 128), 0)
    spread = jnp.zeros((columns, 128), jnp.float32)
    for k, product in enumerate((r * r, d * image, r * image, image * image)):
        spread = jnp.where(lane == sub + k * columns, jnp.sum(product, 1, keepdims=True), spread)
    mine[...] = jnp.sum(spread, 0, keepdims=True)

    def sum_copy(k):
        return pltpu.make_async_remote_copy(
            src_ref=mine,
            dst_ref=sums.at[k],
            send_sem=sum_send.at[k],
            recv_sem=sum_recv.at[k],
            device_id={"row": (me + k) % n},
            device_id_type=pl.DeviceIdType.MESH,
        )

    def send_sum(k, carry):
        sum_copy(k).start()
        return carry

    lax.fori_loop(1, n, send_sum, 0)
    sums[0] = mine[...]

    def drain(k, carry):
        copy(0, k, sibling).wait_send()
        return carry

    lax.fori_loop(1, n, drain, 0)

    def take_sum(k, carry):
        sum_copy(k).wait()
        return carry

    lax.fori_loop(1, n, take_sum, 0)
    whole = jnp.broadcast_to(jnp.sum(sums[...], 0), (columns, 128))
    rr, curv, ri, ii = (
        jnp.sum(jnp.where(lane == sub + k * columns, whole, 0.0), 1, keepdims=True)
        for k in range(4)
    )
    alpha = rr / curv
    rr_new = jnp.maximum(rr - 2.0 * alpha * ri + alpha * alpha * ii, 0.0)
    image_out[...] = image
    rates_out[...] = jnp.where(lane == 0, alpha, rr_new / rr)


def shards(n, depth, features, inv_length, outscale, noise_var, solution, residual, direction):
    feats, points = features.shape
    columns = direction.shape[0]
    hbm = pl.BlockSpec(memory_space=pltpu.HBM)
    vmem = pl.BlockSpec(memory_space=pltpu.VMEM)
    image, rates = pl.pallas_call(
        functools.partial(step_kernel, n, depth),
        out_shape=(
            jax.ShapeDtypeStruct(direction.shape, jnp.float32),
            jax.ShapeDtypeStruct((columns, 128), jnp.float32),
        ),
        in_specs=[hbm] * 6,
        out_specs=(vmem, vmem),
        scratch_shapes=[
            pltpu.VMEM((feats, points), jnp.float32),
            pltpu.SMEM((feats,), jnp.float32),
            pltpu.SMEM((1,), jnp.float32),
            pltpu.SMEM((1,), jnp.float32),
            pltpu.VMEM((columns, points), jnp.float32),
            pltpu.VMEM((n, feats + columns, points), jnp.float32),
            pltpu.VMEM((8 * feats, points), jnp.bfloat16),
            pltpu.VMEM((2 * columns, points), jnp.float32),
            pltpu.VMEM((1, 128), jnp.float32),
            pltpu.VMEM((n, 1, 128), jnp.float32),
            pltpu.SemaphoreType.DMA((n,)),
            pltpu.SemaphoreType.DMA((n,)),
            pltpu.SemaphoreType.DMA((n,)),
            pltpu.SemaphoreType.DMA((n,)),
            pltpu.SemaphoreType.DMA((6,)),
        ],
        compiler_params=pltpu.CompilerParams(
            collective_id=0, has_side_effects=True, vmem_limit_bytes=60 * 1024 * 1024
        ),
    )(features, inv_length, outscale, noise_var, residual, direction)
    alpha, beta = rates[:, 0:1], rates[:, 1:2]
    new_residual = residual - alpha * image
    return solution + alpha * direction, new_residual, new_residual + beta * direction


def solution(mesh):
    n = mesh.shape["row"]
    depth = 1
    while 4 * depth * depth <= n // 2:
        depth *= 2
    whole = P(None, ("groups", "row"))
    part = P("groups")
    return jax.shard_map(
        functools.partial(shards, n, depth),
        mesh=mesh,
        in_specs=(whole, part, part, part, whole, whole, whole),
        out_specs=(whole, whole, whole),
        check_vma=False,
    )
```
